512 devices in a mesh: wide: 16 (over y, core), narrow: 32 (over z, x).
Axes of the slice: x: 4, y: 8, z: 8, core: 2. Of those that a mesh axis runs over, the one named last changes fastest.
Arguments:
- embeddings: bfloat16 [12288, 1024], P(('wide', 'narrow')), may hold values from -6 to 6
- cluster: int32 [512], replicated, may hold values from 0 to 44, never falling along the last dimension, each value on 1 to 34 neighbouring positions
Outputs:
- shifted: float32 [12288, 1024], P(('wide', 'narrow'))
The draws below stay inside these ranges and needn't reach their ends.
Inputs may be any that keep to these rules, and one draw needn't show every extreme that they name: The blocks of one cluster are consecutive (ids never fall); each cluster holds 1 to 34 blocks, one exactly 34.
All inputs are finite; a program needn't handle non-finite values.
Results may differ from the reference program's by a relative error of at most 0.029.
Values may be sent and summed in bfloat16 or wider, within the bound.
A program may use at most 64 MiB of HBM per device.

```python
import math
import jax
import jax.numpy as jnp
import numpy as np
from jax import lax

D = 1024
BLK = 24
BLOCKS = 512
ROWS = 12288
MOST = 34
COUNT = 45


def block_scale(stream_key, dims, pieces, least, top_value):
    level = 1.0
    for axis_at, shards_of in pieces:
        heights = jax.random.uniform(jax.random.fold_in(jax.random.fold_in(stream_key, 6), axis_at), (shards_of,), jnp.float32, least / len(pieces), top_value / len(pieces))
        level = level * jnp.repeat(jnp.exp(heights), dims[axis_at] // shards_of).reshape((-1,) + (1,) * (len(dims) - 1 - axis_at))
    return level


def split_up(amount, total, reach, lean):
    portions = [(1 << 20) // math.isqrt(grade ** lean) + 1 for grade in range(2, amount + 1)]
    spare, counts = total - reach - (amount - 1), [1] * (amount - 1)
    while spare > 0:
        free = [i for i in range(amount - 1) if counts[i] < reach]
        whole, left = sum([portions[i] for i in free]), spare
        for i in free:
            extra = min(reach - counts[i], max(1, left * portions[i] // whole), spare)
            counts[i] = counts[i] + extra
            spare = spare - extra
    return np.array([reach] + counts)


def ragged(own_key, amount, total, most, lean):
    if amount == 2:
        one = jax.random.randint(own_key, (), max(1, total - most), min(most, total - 1) + 1)
        return jnp.stack([one, total - one])
    lengths = jnp.asarray(split_up(amount, total, most, lean), jnp.int32)
    couples = (amount - 1) // 2
    donor, sink = lengths[1:1 + 2 * couples:2], lengths[2:2 + 2 * couples:2]
    slack = jnp.minimum(donor - 1, most - sink)
    passed = jax.random.randint(jax.random.fold_in(own_key, 1), (couples,), 0, 1 << 20) % (slack + 1)
    lengths = lengths.at[1:1 + 2 * couples:2].set(donor - passed).at[2:2 + 2 * couples:2].set(sink + passed)
    return lengths[jax.random.permutation(jax.random.fold_in(own_key, 2), amount)]


def bell_draw(key, shape, spread, bound, cuts=(), held_as=jnp.bfloat16):
    values = jax.random.normal(key, shape, jnp.float32) * spread
    if len(cuts) > 0:
        values = block_scale(key, shape, cuts, -0.22, 0.18) * values
    return jnp.clip(values, min=-bound, max=bound).astype(held_as)


def setup_inputs(seed: int = 0) -> dict:
    key_of = jax.random.split(jax.random.key(seed), 3)
    return {
        "embeddings": bell_draw(key_of[0], (ROWS, D), 1.0, 6.0, ((0, 512),)),
        "cluster": jnp.searchsorted(jnp.cumsum(ragged(key_of[1], COUNT, BLOCKS, MOST, 2)), jnp.arange(BLOCKS), side="right").astype(jnp.int32),
    }


SPREAD = 0.5

def normalize(rows):
    values = rows.astype(jnp.float32)
    factor = lax.rsqrt(lax.optimization_barrier(jnp.mean(values * values, axis=1, keepdims=True)) + 1e-06)
    return (values * factor).astype(jnp.bfloat16)

def reference(embeddings, cluster):
    normed = normalize(embeddings)
    span = MOST - 1
    blocks = normed.reshape(BLOCKS, BLK, D)
    padding = jnp.zeros((span, BLK, D), jnp.bfloat16)
    padded = jnp.concatenate([padding, blocks, padding], axis=0)
    fill = jnp.full((span,), -1, jnp.int32)
    padded_cluster = jnp.concatenate([fill, cluster.astype(jnp.int32), fill], axis=0)
    offsets = jnp.arange(-span, span + 1).astype(jnp.int32)
    scale = 1.0 / (SPREAD * math.sqrt(D))
    same_row = jnp.arange(BLK)[:, None] == jnp.arange(BLK)[None, :]

    def one_block(index):
        query = lax.dynamic_index_in_dim(blocks, index, 0, keepdims=False)
        mine = lax.dynamic_index_in_dim(cluster.astype(jnp.int32), index, 0, keepdims=False)

        def step(carry, offset):
            numerator, total = carry
            where_at = (index + offset + span).astype(jnp.int32)

            def compute(unused):
                keys = lax.dynamic_index_in_dim(padded, where_at, 0, keepdims=False)
                scores = lax.dot_general(query, keys, (((1,), (1,)), ((), ())), preferred_element_type=jnp.float32)
                weights = jnp.exp(scores * scale)
                weights = jnp.where(same_row & (offset == 0), jnp.float32(0.0), weights)
                added = jnp.dot(weights.astype(jnp.bfloat16), keys, preferred_element_type=jnp.float32)
                return (numerator + added, total + lax.optimization_barrier(jnp.sum(weights, axis=1)))

            def unchanged(unused):
                return (numerator, total)
            other = lax.dynamic_index_in_dim(padded_cluster, where_at, 0, keepdims=False)
            return (lax.cond(other == mine, compute, unchanged, 0), None)
        start = (jnp.zeros((BLK, D), jnp.float32), jnp.zeros((BLK,), jnp.float32))
        (numerator, total), unused = lax.scan(step, start, offsets)
        return numerator / total[:, None]
    result = lax.map(one_block, jnp.arange(BLOCKS).astype(jnp.int32))
    return result.reshape(ROWS, D)
```

```python
import functools
import math

import jax
import jax.numpy as jnp
from jax import lax
from jax.experimental import pallas as pl
from jax.experimental.pallas import tpu as pltpu
from jax.sharding import PartitionSpec as P

D = 1024
BLK = 24
BLOCKS = 512
REACH = 33
SPREAD = 0.5
LANES = 128
MESH = pl.DeviceIdType.MESH

MARKS = (0, 27, 30, 29, 24, 12, 8, -2, -1, 1, 32)
COUNT = len(MARKS)
WIDTH = D + LANES


def pair_bits():
    bits = [0] * COUNT
    bits[0] |= 1
    for gap in range(1, REACH + 1):
        k, l = next(
            (k, l)
            for k in range(COUNT)
            for l in range(COUNT)
            if MARKS[l] - MARKS[k] == gap
        )
        bits[l] |= 1 << k
        bits[k] |= 1 << l
    return bits


def kernel(x_hbm, cluster_hbm, out_ref, raw, cluster, rows, parts, got, in_sem, send1, recv1, send2, recv2):
    n_narrow = lax.axis_size("narrow")
    me = lax.axis_index("wide") * n_narrow + lax.axis_index("narrow")

    def block_at(offset):
        return lax.rem(me + (offset % BLOCKS), BLOCKS)

    def device(offset):
        block = block_at(offset)
        return (lax.div(block, n_narrow), lax.rem(block, n_narrow))

    load = pltpu.make_async_copy(x_hbm, raw, in_sem.at[0])
    load.start()
    load_ids = pltpu.make_async_copy(cluster_hbm, cluster, in_sem.at[1])
    load_ids.start()

    barrier = pltpu.get_barrier_semaphore()
    for k in range(1, COUNT):
        pl.semaphore_signal(barrier, inc=1, device_id=device(MARKS[k]), device_id_type=MESH)

    load.wait()
    values = raw[...].astype(jnp.float32)
    factor = lax.rsqrt(jnp.mean(values * values, axis=1, keepdims=True) + 1e-06)
    rows[0, :, :D] = (values * factor).astype(jnp.bfloat16)
    rows[:, :, D:] = jnp.ones((COUNT, BLK, LANES), jnp.bfloat16)

    pl.semaphore_wait(barrier, COUNT - 1)
    gather = []
    for k in range(1, COUNT):
        copy = pltpu.make_async_remote_copy(
            src_ref=rows.at[0, :, pl.ds(0, D)],
            dst_ref=rows.at[k, :, pl.ds(0, D)],
            send_sem=send1.at[k],
            recv_sem=recv1.at[k],
            device_id=device(-MARKS[k]),
            device_id_type=MESH,
        )
        copy.start()
        gather.append(copy)

    load_ids.wait()
    total_rows = COUNT * BLK
    lane = lax.broadcasted_iota(jnp.int32, (BLK, total_rows), 1)
    sub = lax.broadcasted_iota(jnp.int32, (BLK, total_rows), 0)
    ids = [cluster[block_at(s)] for s in MARKS]
    bits = pair_bits()
    lane_id = jnp.full((BLK, total_rows), ids[0], jnp.int32)
    lane_bits = jnp.full((BLK, total_rows), bits[0], jnp.int32)
    for l in range(1, COUNT):
        later = lane >= l * BLK
        lane_id = jnp.where(later, ids[l], lane_id)
        lane_bits = jnp.where(later, bits[l], lane_bits)

    for copy in gather:
        copy.wait_recv()

    keys = rows[...].reshape(total_rows, WIDTH)
    scores = lax.dot_general(
        keys[:, :D], keys[:, :D], (((1,), (1,)), ((), ())), preferred_element_type=jnp.float32
    )
    tiles = []
    for k in range(COUNT):
        keep = (lane_id == ids[k]) & ((lane_bits & (1 << k)) != 0)
        if k == 0:
            keep = keep & (lane != sub)
        weights = jnp.exp(scores[k * BLK : (k + 1) * BLK] * (1.0 / (SPREAD * math.sqrt(D))))
        tiles.append(jnp.where(keep, weights, 0.0).astype(jnp.bfloat16))
    sums = jnp.dot(jnp.concatenate(tiles, axis=0), keys, preferred_element_type=jnp.float32)

    back = []
    for k in range(1, COUNT):
        parts[k] = sums[k * BLK : (k + 1) * BLK].astype(jnp.bfloat16)
        copy = pltpu.make_async_remote_copy(
            src_ref=parts.at[k],
            dst_ref=got.at[k],
            send_sem=send2.at[k],
            recv_sem=recv2.at[k],
            device_id=device(MARKS[k]),
            device_id_type=MESH,
        )
        copy.start()
        back.append(copy)

    for copy in gather:
        copy.wait_send()
    own = sums[:BLK]
    for copy in back:
        copy.wait_recv()
    for k in range(1, COUNT):
        own = own + got[k].astype(jnp.float32)
    inverse = 1.0 / own[:, D:]
    for c in range(D // LANES):
        out_ref[:, c * LANES : (c + 1) * LANES] = own[:, c * LANES : (c + 1) * LANES] * inverse
    for copy in back:
        copy.wait_send()


def on_device(embeddings, cluster):
    return pl.pallas_call(
        kernel,
        out_shape=jax.ShapeDtypeStruct((BLK, D), jnp.float32),
        in_specs=[pl.BlockSpec(memory_space=pl.ANY), pl.BlockSpec(memory_space=pl.ANY)],
        out_specs=pl.BlockSpec(memory_space=pltpu.VMEM),
        scratch_shapes=[
            pltpu.VMEM((BLK, D), jnp.bfloat16),
            pltpu.SMEM((BLOCKS,), jnp.int32),
            pltpu.VMEM((COUNT, BLK, WIDTH), jnp.bfloat16),
            pltpu.VMEM((COUNT, BLK, WIDTH), jnp.bfloat16),
            pltpu.VMEM((COUNT, BLK, WIDTH), jnp.bfloat16),
            pltpu.SemaphoreType.DMA((2,)),
            pltpu.SemaphoreType.DMA((COUNT,)),
            pltpu.SemaphoreType.DMA((COUNT,)),
            pltpu.SemaphoreType.DMA((COUNT,)),
            pltpu.SemaphoreType.DMA((COUNT,)),
        ],
        compiler_params=pltpu.CompilerParams(
            collective_id=0, has_side_effects=True, vmem_limit_bytes=32 * 1024 * 1024
        ),
        name="shift",
    )(embeddings, cluster)


def solution(mesh):
    in_specs = (P(("wide", "narrow"), None), P())
    out_specs = P(("wide", "narrow"), None)
    return jax.shard_map(
        on_device, mesh=mesh, in_specs=in_specs, out_specs=out_specs, check_vma=False
    )
```

```python
import functools
import math

import jax
import jax.numpy as jnp
from jax import lax
from jax.experimental import pallas as pl
from jax.experimental.pallas import tpu as pltpu
from jax.sharding import PartitionSpec as P

D = 1024
BLK = 24
BLOCKS = 512
REACH = 33
SPREAD = 0.5
LANES = 128
MESH = pl.DeviceIdType.MESH

MARKS = (0, 4, 13, 21, -28, -3, -2, 31, -1, 1, 32)
COUNT = len(MARKS)
WIDTH = D + LANES


def pair_bits():
    bits = [0] * COUNT
    bits[0] |= 1
    for gap in range(1, REACH + 1):
        k, l = next(
            (k, l)
            for k in range(COUNT)
            for l in range(COUNT)
            if MARKS[l] - MARKS[k] == gap
        )
        bits[l] |= 1 << k
        bits[k] |= 1 << l
    return bits


def kernel(x_hbm, cluster_hbm, out_ref, raw, cluster, rows, parts, got, in_sem, send1, recv1, send2, recv2):
    n_narrow = lax.axis_size("narrow")
    me = lax.axis_index("wide") * n_narrow + lax.axis_index("narrow")

    def block_at(offset):
        return lax.rem(me + (offset % BLOCKS), BLOCKS)

    def device(offset):
        block = block_at(offset)
        return (lax.div(block, n_narrow), lax.rem(block, n_narrow))

    load = pltpu.make_async_copy(x_hbm, raw, in_sem.at[0])
    load.start()
    load_ids = pltpu.make_async_copy(cluster_hbm, cluster, in_sem.at[1])
    load_ids.start()

    barrier = pltpu.get_barrier_semaphore()
    for k in range(1, COUNT):
        pl.semaphore_signal(barrier, inc=1, device_id=device(MARKS[k]), device_id_type=MESH)

    load.wait()
    values = raw[...].astype(jnp.float32)
    factor = lax.rsqrt(jnp.mean(values * values, axis=1, keepdims=True) + 1e-06)
    rows[0, :, :D] = (values * factor).astype(jnp.bfloat16)
    rows[:, :, D:] = jnp.ones((COUNT, BLK, LANES), jnp.bfloat16)

    pl.semaphore_wait(barrier, COUNT - 1)
    gather = []
    for k in range(1, COUNT):
        copy = pltpu.make_async_remote_copy(
            src_ref=rows.at[0, :, pl.ds(0, D)],
            dst_ref=rows.at[k, :, pl.ds(0, D)],
            send_sem=send1.at[k],
            recv_sem=recv1.at[k],
            device_id=device(-MARKS[k]),
            device_id_type=MESH,
        )
        copy.start()
        gather.append(copy)

    load_ids.wait()
    total_rows = COUNT * BLK
    lane = lax.broadcasted_iota(jnp.int32, (BLK, total_rows), 1)
    sub = lax.broadcasted_iota(jnp.int32, (BLK, total_rows), 0)
    ids = [cluster[block_at(s)] for s in MARKS]
    bits = pair_bits()
    lane_id = jnp.full((BLK, total_rows), ids[0], jnp.int32)
    lane_bits = jnp.full((BLK, total_rows), bits[0], jnp.int32)
    for l in range(1, COUNT):
        later = lane >= l * BLK
        lane_id = jnp.where(later, ids[l], lane_id)
        lane_bits = jnp.where(later, bits[l], lane_bits)

    for copy in gather:
        copy.wait_recv()

    keys = rows[...].reshape(total_rows, WIDTH)
    scores = lax.dot_general(
        keys[:, :D], keys[:, :D], (((1,), (1,)), ((), ())), preferred_element_type=jnp.float32
    )
    tiles = []
    for k in range(COUNT):
        keep = (lane_id == ids[k]) & ((lane_bits & (1 << k)) != 0)
        if k == 0:
            keep = keep & (lane != sub)
        weights = jnp.exp(scores[k * BLK : (k + 1) * BLK] * (1.0 / (SPREAD * math.sqrt(D))))
        tiles.append(jnp.where(keep, weights, 0.0).astype(jnp.bfloat16))
    sums = jnp.dot(jnp.concatenate(tiles, axis=0), keys, preferred_element_type=jnp.float32)

    back = []
    for k in range(1, COUNT):
        parts[k] = sums[k * BLK : (k + 1) * BLK].astype(jnp.bfloat16)
        copy = pltpu.make_async_remote_copy(
            src_ref=parts.at[k],
            dst_ref=got.at[k],
            send_sem=send2.at[k],
            recv_sem=recv2.at[k],
            device_id=device(MARKS[k]),
            device_id_type=MESH,
        )
        back.append(copy)
    for low, high in ((0, 2), (2, 4), (4, 8)):
        for k in range(1, COUNT):
            z = lax.rem(lax.div(block_at(MARKS[k]), 4), 8)

            @pl.when((z >= low) & (z < high))
            def _():
                back[k - 1].start()


    for copy in gather:
        copy.wait_send()
    own = sums[:BLK]
    for copy in back:
        copy.wait_recv()
    for k in range(1, COUNT):
        own = own + got[k].astype(jnp.float32)
    inverse = 1.0 / own[:, D:]
    for c in range(D // LANES):
        out_ref[:, c * LANES : (c + 1) * LANES] = own[:, c * LANES : (c + 1) * LANES] * inverse
    for copy in back:
        copy.wait_send()


def on_device(embeddings, cluster):
    return pl.pallas_call(
        kernel,
        out_shape=jax.ShapeDtypeStruct((BLK, D), jnp.float32),
        in_specs=[pl.BlockSpec(memory_space=pltpu.HBM), pl.BlockSpec(memory_space=pltpu.HBM)],
        out_specs=pl.BlockSpec(memory_space=pltpu.VMEM),
        scratch_shapes=[
            pltpu.VMEM((BLK, D), jnp.bfloat16),
            pltpu.SMEM((BLOCKS,), jnp.int32),
            pltpu.VMEM((COUNT, BLK, WIDTH), jnp.bfloat16),
            pltpu.VMEM((COUNT, BLK, WIDTH), jnp.bfloat16),
            pltpu.VMEM((COUNT, BLK, WIDTH), jnp.bfloat16),
            pltpu.SemaphoreType.DMA((2,)),
            pltpu.SemaphoreType.DMA((COUNT,)),
            pltpu.SemaphoreType.DMA((COUNT,)),
            pltpu.SemaphoreType.DMA((COUNT,)),
            pltpu.SemaphoreType.DMA((COUNT,)),
        ],
        compiler_params=pltpu.CompilerParams(
            collective_id=0, has_side_effects=True, vmem_limit_bytes=32 * 1024 * 1024
        ),
        name="shift",
    )(pltpu.with_memory_space_constraint(embeddings, pltpu.HBM), pltpu.with_memory_space_constraint(cluster, pltpu.HBM))


def solution(mesh):
    in_specs = (P(("wide", "narrow"), None), P())
    out_specs = P(("wide", "narrow"), None)
    return jax.shard_map(
        on_device, mesh=mesh, in_specs=in_specs, out_specs=out_specs, check_vma=False
    )
```

```python
import functools
import math

import jax
import jax.numpy as jnp
from jax import lax
from jax.experimental import pallas as pl
from jax.experimental.pallas import tpu as pltpu
from jax.sharding import PartitionSpec as P

D = 1024
BLK = 24
BLOCKS = 512
REACH = 33
SPREAD = 0.5
LANES = 128
MESH = pl.DeviceIdType.MESH

ROW = 4
GROUPS = BLOCKS // ROW
MARKS = ((0, 0), (-6, 1), (3, 0), (-2, 3), (7, 3), (0, 2), (-1, 3), (0, 3), (0, 1), (-1, 0), (8, 0))
COUNT = len(MARKS)
WIDTH = D + LANES


def slots(a, b):
    return next(
        (k, l)
        for k in range(COUNT)
        for l in range(COUNT)
        if k != l and MARKS[l][0] - MARKS[k][0] == a and (MARKS[l][1] - MARKS[k][1]) % ROW == b
    )


def pair_bits(place):
    pairs = [slots(0, 1)]
    for a in range(1, REACH // ROW + 2):
        for b in range(ROW):
            if any(ROW * a + y - x <= REACH for x in range(ROW) for y in range(ROW) if (y - x) % ROW == b):
                pairs.append(slots(a, b))
    bits = [0] * COUNT
    bits[0] |= 1
    for k, l in pairs:
        bits[l] |= 1 << k
        bits[k] |= 1 << l
    k, l = slots(0, 2)
    low = (place + MARKS[k][1]) % ROW < ROW // 2
    bits[l] = bits[l] + jnp.where(low, 1 << k, 0)
    bits[k] = bits[k] + jnp.where(low, 1 << l, 0)
    return bits


def kernel(x_hbm, cluster_hbm, out_ref, raw, cluster, rows, parts, got, in_sem, send1, recv1, send2, recv2):
    n_narrow = lax.axis_size("narrow")
    me = lax.axis_index("wide") * n_narrow + lax.axis_index("narrow")

    def block_at(mark, way=1):
        group = (me // ROW + way * mark[0] + GROUPS) % GROUPS
        return group * ROW + (me + way * mark[1] + ROW) % ROW

    def device(mark, way=1):
        block = block_at(mark, way)
        return (block // n_narrow, block % n_narrow)

    load = pltpu.make_async_copy(x_hbm, raw, in_sem.at[0])
    load.start()
    load_ids = pltpu.make_async_copy(cluster_hbm, cluster, in_sem.at[1])
    load_ids.start()

    barrier = pltpu.get_barrier_semaphore()
    for k in range(1, COUNT):
        pl.semaphore_signal(barrier, inc=1, device_id=device(MARKS[k]), device_id_type=MESH)

    load.wait()
    values = raw[...].astype(jnp.float32)
    factor = lax.rsqrt(jnp.mean(values * values, axis=1, keepdims=True) + 1e-06)
    rows[0, :, :D] = (values * factor).astype(jnp.bfloat16)
    rows[:, :, D:] = jnp.ones((COUNT, BLK, LANES), jnp.bfloat16)

    pl.semaphore_wait(barrier, COUNT - 1)
    gather = []
    for k in range(1, COUNT):
        copy = pltpu.make_async_remote_copy(
            src_ref=rows.at[0, :, pl.ds(0, D)],
            dst_ref=rows.at[k, :, pl.ds(0, D)],
            send_sem=send1.at[k],
            recv_sem=recv1.at[k],
            device_id=device(MARKS[k], -1),
            device_id_type=MESH,
        )
        copy.start()
        gather.append(copy)

    load_ids.wait()
    total_rows = COUNT * BLK
    lane = lax.broadcasted_iota(jnp.int32, (BLK, total_rows), 1)
    sub = lax.broadcasted_iota(jnp.int32, (BLK, total_rows), 0)
    ids = [cluster[block_at(s)] for s in MARKS]
    bits = pair_bits(me % ROW)
    lane_id = jnp.full((BLK, total_rows), ids[0], jnp.int32)
    lane_bits = jnp.full((BLK, total_rows), bits[0], jnp.int32)
    for l in range(1, COUNT):
        later = lane >= l * BLK
        lane_id = jnp.where(later, ids[l], lane_id)
        lane_bits = jnp.where(later, bits[l], lane_bits)

    for copy in gather:
        copy.wait_recv()

    keys = rows[...].reshape(total_rows, WIDTH)
    scores = lax.dot_general(
        keys[:, :D], keys[:, :D], (((1,), (1,)), ((), ())), preferred_element_type=jnp.float32
    )
    tiles = []
    for k in range(COUNT):
        keep = (lane_id == ids[k]) & ((lane_bits & (1 << k)) != 0)
        if k == 0:
            keep = keep & (lane != sub)
        weights = jnp.exp(scores[k * BLK : (k + 1) * BLK] * (1.0 / (SPREAD * math.sqrt(D))))
        tiles.append(jnp.where(keep, weights, 0.0).astype(jnp.bfloat16))
    sums = jnp.dot(jnp.concatenate(tiles, axis=0), keys, preferred_element_type=jnp.float32)

    back = []
    for k in range(1, COUNT):
        parts[k] = sums[k * BLK : (k + 1) * BLK].astype(jnp.bfloat16)
        copy = pltpu.make_async_remote_copy(
            src_ref=parts.at[k],
            dst_ref=got.at[k],
            send_sem=send2.at[k],
            recv_sem=recv2.at[k],
            device_id=device(MARKS[k]),
            device_id_type=MESH,
        )
        back.append(copy)
    for low, high in ((0, 2), (2, 4), (4, 8)):
        for k in range(1, COUNT):
            z = block_at(MARKS[k]) % n_narrow // ROW

            @pl.when((z >= low) & (z < high))
            def _():
                back[k - 1].start()


    for copy in gather:
        copy.wait_send()
    own = sums[:BLK]
    for copy in back:
        copy.wait_recv()
    for k in range(1, COUNT):
        own = own + got[k].astype(jnp.float32)
    inverse = 1.0 / own[:, D:]
    for c in range(D // LANES):
        out_ref[:, c * LANES : (c + 1) * LANES] = own[:, c * LANES : (c + 1) * LANES] * inverse
    for copy in back:
        copy.wait_send()


def on_device(embeddings, cluster):
    return pl.pallas_call(
        kernel,
        out_shape=jax.ShapeDtypeStruct((BLK, D), jnp.float32),
        in_specs=[pl.BlockSpec(memory_space=pltpu.HBM), pl.BlockSpec(memory_space=pltpu.HBM)],
        out_specs=pl.BlockSpec(memory_space=pltpu.VMEM),
        scratch_shapes=[
            pltpu.VMEM((BLK, D), jnp.bfloat16),
            pltpu.SMEM((BLOCKS,), jnp.int32),
            pltpu.VMEM((COUNT, BLK, WIDTH), jnp.bfloat16),
            pltpu.VMEM((COUNT, BLK, WIDTH), jnp.bfloat16),
            pltpu.VMEM((COUNT, BLK, WIDTH), jnp.bfloat16),
            pltpu.SemaphoreType.DMA((2,)),
            pltpu.SemaphoreType.DMA((COUNT,)),
            pltpu.SemaphoreType.DMA((COUNT,)),
            pltpu.SemaphoreType.DMA((COUNT,)),
            pltpu.SemaphoreType.DMA((COUNT,)),
        ],
        compiler_params=pltpu.CompilerParams(
            collective_id=0, has_side_effects=True, vmem_limit_bytes=32 * 1024 * 1024
        ),
        name="shift",
    )(pltpu.with_memory_space_constraint(embeddings, pltpu.HBM), pltpu.with_memory_space_constraint(cluster, pltpu.HBM))


def solution(mesh):
    in_specs = (P(("wide", "narrow"), None), P())
    out_specs = P(("wide", "narrow"), None)
    return jax.shard_map(
        on_device, mesh=mesh, in_specs=in_specs, out_specs=out_specs, check_vma=False
    )
```

```python
import functools
import math

import jax
import jax.numpy as jnp
from jax import lax
from jax.experimental import pallas as pl
from jax.experimental.pallas import tpu as pltpu
from jax.sharding import PartitionSpec as P

D = 1024
BLK = 24
BLOCKS = 512
REACH = 33
SPREAD = 0.5
LANES = 128
MESH = pl.DeviceIdType.MESH

ROW = 4
GROUPS = BLOCKS // ROW
MARKS = ((0, 0), (-6, 1), (3, 0), (-2, 3), (7, 3), (0, 2), (-1, 3), (0, 3), (0, 1), (-1, 0), (8, 0))
COUNT = len(MARKS)
SUBLANES = 8
ROW_TILES, LANE_TILES = BLK // SUBLANES, D // LANES
TILES = ROW_TILES * LANE_TILES + 1


def slots(a, b):
    return next(
        (k, l)
        for k in range(COUNT)
        for l in range(COUNT)
        if k != l and MARKS[l][0] - MARKS[k][0] == a and (MARKS[l][1] - MARKS[k][1]) % ROW == b
    )


def pair_bits(place):
    pairs = [slots(0, 1)]
    for a in range(1, REACH // ROW + 2):
        for b in range(ROW):
            if any(ROW * a + y - x <= REACH for x in range(ROW) for y in range(ROW) if (y - x) % ROW == b):
                pairs.append(slots(a, b))
    bits = [0] * COUNT
    bits[0] |= 1
    for k, l in pairs:
        bits[l] |= 1 << k
        bits[k] |= 1 << l
    k, l = slots(0, 2)
    low = (place + MARKS[k][1]) % ROW < ROW // 2
    bits[l] = bits[l] + jnp.where(low, 1 << k, 0)
    bits[k] = bits[k] + jnp.where(low, 1 << l, 0)
    return bits


def kernel(x_hbm, cluster_hbm, out_ref, raw, cluster, rows, parts, got, in_sem, send1, recv1, send2, recv2):
    n_narrow = lax.axis_size("narrow")
    me = lax.axis_index("wide") * n_narrow + lax.axis_index("narrow")

    def block_at(mark, way=1):
        group = (me // ROW + way * mark[0] + GROUPS) % GROUPS
        return group * ROW + (me + way * mark[1] + ROW) % ROW

    def device(mark, way=1):
        block = block_at(mark, way)
        return (block // n_narrow, block % n_narrow)

    load = pltpu.make_async_copy(x_hbm, raw, in_sem.at[0])
    load.start()
    load_ids = pltpu.make_async_copy(cluster_hbm, cluster, in_sem.at[1])
    load_ids.start()

    barrier = pltpu.get_barrier_semaphore()
    for k in range(1, COUNT):
        pl.semaphore_signal(barrier, inc=1, device_id=device(MARKS[k]), device_id_type=MESH)

    load.wait()
    values = raw[...].astype(jnp.float32)
    factor = lax.rsqrt(jnp.mean(values * values, axis=1, keepdims=True) + 1e-06)
    rows[0] = (values * factor).astype(jnp.bfloat16)

    pl.semaphore_wait(barrier, COUNT - 1)
    gather = []
    for k in range(1, COUNT):
        copy = pltpu.make_async_remote_copy(
            src_ref=rows.at[0],
            dst_ref=rows.at[k],
            send_sem=send1.at[k],
            recv_sem=recv1.at[k],
            device_id=device(MARKS[k], -1),
            device_id_type=MESH,
        )
        copy.start()
        gather.append(copy)

    load_ids.wait()
    total_rows = COUNT * BLK
    lane = lax.broadcasted_iota(jnp.int32, (BLK, total_rows), 1)
    sub = lax.broadcasted_iota(jnp.int32, (BLK, total_rows), 0)
    ids = [cluster[block_at(s)] for s in MARKS]
    bits = pair_bits(me % ROW)
    lane_id = jnp.full((BLK, total_rows), ids[0], jnp.int32)
    lane_bits = jnp.full((BLK, total_rows), bits[0], jnp.int32)
    for l in range(1, COUNT):
        later = lane >= l * BLK
        lane_id = jnp.where(later, ids[l], lane_id)
        lane_bits = jnp.where(later, bits[l], lane_bits)

    for copy in gather:
        copy.wait_recv()

    keys = rows[...].reshape(total_rows, D)
    column = lax.broadcasted_iota(jnp.int32, (SUBLANES, LANES), 1)
    ones = jnp.ones((total_rows, LANES), jnp.bfloat16)

    def partials(first, last):
        scores = lax.dot_general(
            keys[first * BLK : last * BLK],
            keys,
            (((1,), (1,)), ((), ())),
            preferred_element_type=jnp.float32,
        )
        tiles = []
        for k in range(first, last):
            keep = (lane_id == ids[k]) & ((lane_bits & (1 << k)) != 0)
            if k == 0:
                keep = keep & (lane != sub)
            at = (k - first) * BLK
            weights = jnp.exp(scores[at : at + BLK] * (1.0 / (SPREAD * math.sqrt(D))))
            tiles.append(jnp.where(keep, weights, 0.0).astype(jnp.bfloat16))
        rounded = jnp.concatenate(tiles, axis=0)
        sums = jnp.dot(rounded, keys, preferred_element_type=jnp.float32)
        totals = jnp.dot(rounded, ones, preferred_element_type=jnp.float32)
        found = []
        for k in range(first, last):
            starts = [(k - first) * BLK + SUBLANES * r for r in range(ROW_TILES)]
            total = totals[starts[0] : starts[0] + SUBLANES]
            for r in range(1, ROW_TILES):
                total = jnp.where(column == r, totals[starts[r] : starts[r] + SUBLANES], total)
            numerator = [
                sums[at : at + SUBLANES, c * LANES : (c + 1) * LANES]
                for at in starts
                for c in range(LANE_TILES)
            ]
            found.append(numerator + [total])
        return found

    back = []
    for first, last in ((1, 6), (6, COUNT)):
        for k, found in enumerate(partials(first, last), first):
            for t, tile in enumerate(found):
                parts[k, t] = tile.astype(jnp.bfloat16)
            copy = pltpu.make_async_remote_copy(
                src_ref=parts.at[k],
                dst_ref=got.at[k],
                send_sem=send2.at[k],
                recv_sem=recv2.at[k],
                device_id=device(MARKS[k]),
                device_id_type=MESH,
            )
            copy.start()
            back.append(copy)
    own = partials(0, 1)[0]

    for copy in gather:
        copy.wait_send()
    for k in reversed(range(1, COUNT)):
        back[k - 1].wait_recv()
        own = [tile + got[k, t].astype(jnp.float32) for t, tile in enumerate(own)]
    inverse = 1.0 / own[-1]
    for r in range(ROW_TILES):
        for c in range(LANE_TILES):
            out_ref[r * SUBLANES : (r + 1) * SUBLANES, c * LANES : (c + 1) * LANES] = (
                own[r * LANE_TILES + c] * inverse[:, r : r + 1]
            )
    for copy in back:
        copy.wait_send()


def on_device(embeddings, cluster):
    return pl.pallas_call(
        kernel,
        out_shape=jax.ShapeDtypeStruct((BLK, D), jnp.float32),
        in_specs=[pl.BlockSpec(memory_space=pltpu.HBM), pl.BlockSpec(memory_space=pltpu.HBM)],
        out_specs=pl.BlockSpec(memory_space=pltpu.VMEM),
        scratch_shapes=[
            pltpu.VMEM((BLK, D), jnp.bfloat16),
            pltpu.SMEM((BLOCKS,), jnp.int32),
            pltpu.VMEM((COUNT, BLK, D), jnp.bfloat16),
            pltpu.VMEM((COUNT, TILES, SUBLANES, LANES), jnp.bfloat16),
            pltpu.VMEM((COUNT, TILES, SUBLANES, LANES), jnp.bfloat16),
            pltpu.SemaphoreType.DMA((2,)),
            pltpu.SemaphoreType.DMA((COUNT,)),
            pltpu.SemaphoreType.DMA((COUNT,)),
            pltpu.SemaphoreType.DMA((COUNT,)),
            pltpu.SemaphoreType.DMA((COUNT,)),
        ],
        compiler_params=pltpu.CompilerParams(
            collective_id=0, has_side_effects=True, vmem_limit_bytes=32 * 1024 * 1024
        ),
        name="shift",
    )(pltpu.with_memory_space_constraint(embeddings, pltpu.HBM), pltpu.with_memory_space_constraint(cluster, pltpu.HBM))


def solution(mesh):
    in_specs = (P(("wide", "narrow"), None), P())
    out_specs = P(("wide", "narrow"), None)
    return jax.shard_map(
        on_device, mesh=mesh, in_specs=in_specs, out_specs=out_specs, check_vma=False
    )
```

```python
import functools
import math

import jax
import jax.numpy as jnp
from jax import lax
from jax.experimental import pallas as pl
from jax.experimental.pallas import tpu as pltpu
from jax.sharding import PartitionSpec as P

D = 1024
BLK = 24
BLOCKS = 512
REACH = 33
SPREAD = 0.5
LANES = 128
MESH = pl.DeviceIdType.MESH

ROW = 4
GROUPS = BLOCKS // ROW
MARKS = ((0, 0), (-6, 1), (3, 0), (-2, 3), (7, 3), (0, 2), (-1, 3), (0, 3), (0, 1), (-1, 0), (8, 0))
COUNT = len(MARKS)
SUBLANES = 8
ROW_TILES, LANE_TILES = BLK // SUBLANES, D // LANES
TILES = ROW_TILES * LANE_TILES + 1


def slots(a, b):
    return next(
        (k, l)
        for k in range(COUNT)
        for l in range(COUNT)
        if k != l and MARKS[l][0] - MARKS[k][0] == a and (MARKS[l][1] - MARKS[k][1]) % ROW == b
    )


def pair_bits(place):
    pairs = [slots(0, 1)]
    for a in range(1, REACH // ROW + 2):
        for b in range(ROW):
            if any(ROW * a + y - x <= REACH for x in range(ROW) for y in range(ROW) if (y - x) % ROW == b):
                pairs.append(slots(a, b))
    bits = [0] * COUNT
    bits[0] |= 1
    for k, l in pairs:
        bits[l] |= 1 << k
        bits[k] |= 1 << l
    k, l = slots(0, 2)
    low = (place + MARKS[k][1]) % ROW < ROW // 2
    bits[l] = bits[l] + jnp.where(low, 1 << k, 0)
    bits[k] = bits[k] + jnp.where(low, 1 << l, 0)
    return bits


def kernel(x_hbm, cluster_hbm, out_ref, raw, cluster, rows, parts, got, in_sem, send1, recv1, send2, recv2):
    n_narrow = lax.axis_size("narrow")
    me = lax.axis_index("wide") * n_narrow + lax.axis_index("narrow")

    def block_at(mark, way=1):
        group = (me // ROW + way * mark[0] + GROUPS) % GROUPS
        return group * ROW + (me + way * mark[1] + ROW) % ROW

    def device(mark, way=1):
        block = block_at(mark, way)
        return (block // n_narrow, block % n_narrow)

    barrier = pltpu.get_barrier_semaphore()
    for k in range(1, COUNT):
        pl.semaphore_signal(barrier, inc=1, device_id=device(MARKS[k]), device_id_type=MESH)

    load = pltpu.make_async_copy(x_hbm, raw, in_sem.at[0])
    load.start()
    load_ids = pltpu.make_async_copy(cluster_hbm, cluster, in_sem.at[1])
    load_ids.start()

    load.wait()
    values = raw[...].astype(jnp.float32)
    factor = lax.rsqrt(jnp.mean(values * values, axis=1, keepdims=True) + 1e-06)
    rows[0] = (values * factor).astype(jnp.bfloat16)

    pl.semaphore_wait(barrier, COUNT - 1)
    gather = []
    for k in range(1, COUNT):
        copy = pltpu.make_async_remote_copy(
            src_ref=rows.at[0],
            dst_ref=rows.at[k],
            send_sem=send1.at[k],
            recv_sem=recv1.at[k],
            device_id=device(MARKS[k], -1),
            device_id_type=MESH,
        )
        copy.start()
        gather.append(copy)

    load_ids.wait()
    total_rows = COUNT * BLK
    lane = lax.broadcasted_iota(jnp.int32, (BLK, total_rows), 1)
    sub = lax.broadcasted_iota(jnp.int32, (BLK, total_rows), 0)
    ids = [cluster[block_at(s)] for s in MARKS]
    bits = pair_bits(me % ROW)
    lane_id = jnp.full((BLK, total_rows), ids[0], jnp.int32)
    lane_bits = jnp.full((BLK, total_rows), bits[0], jnp.int32)
    for l in range(1, COUNT):
        later = lane >= l * BLK
        lane_id = jnp.where(later, ids[l], lane_id)
        lane_bits = jnp.where(later, bits[l], lane_bits)

    for copy in gather:
        copy.wait_recv()

    keys = rows[...].reshape(total_rows, D)
    column = lax.broadcasted_iota(jnp.int32, (SUBLANES, LANES), 1)
    ones = jnp.ones((total_rows, LANES), jnp.bfloat16)

    def partials(first, last):
        scores = lax.dot_general(
            keys[first * BLK : last * BLK],
            keys,
            (((1,), (1,)), ((), ())),
            preferred_element_type=jnp.float32,
        )
        tiles = []
        for k in range(first, last):
            keep = (lane_id == ids[k]) & ((lane_bits & (1 << k)) != 0)
            if k == 0:
                keep = keep & (lane != sub)
            at = (k - first) * BLK
            weights = jnp.exp(scores[at : at + BLK] * (1.0 / (SPREAD * math.sqrt(D))))
            tiles.append(jnp.where(keep, weights, 0.0).astype(jnp.bfloat16))
        rounded = jnp.concatenate(tiles, axis=0)
        sums = jnp.dot(rounded, keys, preferred_element_type=jnp.float32)
        totals = jnp.dot(rounded, ones, preferred_element_type=jnp.float32)
        found = []
        for k in range(first, last):
            starts = [(k - first) * BLK + SUBLANES * r for r in range(ROW_TILES)]
            total = totals[starts[0] : starts[0] + SUBLANES]
            for r in range(1, ROW_TILES):
                total = jnp.where(column == r, totals[starts[r] : starts[r] + SUBLANES], total)
            numerator = [
                sums[at : at + SUBLANES, c * LANES : (c + 1) * LANES]
                for at in starts
                for c in range(LANE_TILES)
            ]
            found.append(numerator + [total])
        return found

    back = []
    for first, last in ((1, 8), (8, COUNT)):
        for k, found in enumerate(partials(first, last), first):
            for t, tile in enumerate(found):
                parts[k, t] = tile.astype(jnp.bfloat16)
            copy = pltpu.make_async_remote_copy(
                src_ref=parts.at[k],
                dst_ref=got.at[k],
                send_sem=send2.at[k],
                recv_sem=recv2.at[k],
                device_id=device(MARKS[k]),
                device_id_type=MESH,
            )
            copy.start()
            back.append(copy)
    own = partials(0, 1)[0]

    for copy in gather:
        copy.wait_send()
    for k in reversed(range(1, COUNT)):
        back[k - 1].wait_recv()
        own = [tile + got[k, t].astype(jnp.float32) for t, tile in enumerate(own)]
    inverse = 1.0 / own[-1]
    for r in range(ROW_TILES):
        for c in range(LANE_TILES):
            out_ref[r * SUBLANES : (r + 1) * SUBLANES, c * LANES : (c + 1) * LANES] = (
                own[r * LANE_TILES + c] * inverse[:, r : r + 1]
            )
    for copy in back:
        copy.wait_send()


def on_device(embeddings, cluster):
    return pl.pallas_call(
        kernel,
        out_shape=jax.ShapeDtypeStruct((BLK, D), jnp.float32),
        in_specs=[pl.BlockSpec(memory_space=pltpu.HBM), pl.BlockSpec(memory_space=pltpu.HBM)],
        out_specs=pl.BlockSpec(memory_space=pltpu.VMEM),
        scratch_shapes=[
            pltpu.VMEM((BLK, D), jnp.bfloat16),
            pltpu.SMEM((BLOCKS,), jnp.int32),
            pltpu.VMEM((COUNT, BLK, D), jnp.bfloat16),
            pltpu.VMEM((COUNT, TILES, SUBLANES, LANES), jnp.bfloat16),
            pltpu.VMEM((COUNT, TILES, SUBLANES, LANES), jnp.bfloat16),
            pltpu.SemaphoreType.DMA((2,)),
            pltpu.SemaphoreType.DMA((COUNT,)),
            pltpu.SemaphoreType.DMA((COUNT,)),
            pltpu.SemaphoreType.DMA((COUNT,)),
            pltpu.SemaphoreType.DMA((COUNT,)),
        ],
        compiler_params=pltpu.CompilerParams(
            collective_id=0, has_side_effects=True, vmem_limit_bytes=32 * 1024 * 1024
        ),
        name="shift",
    )(pltpu.with_memory_space_constraint(embeddings, pltpu.HBM), pltpu.with_memory_space_constraint(cluster, pltpu.HBM))


def solution(mesh):
    in_specs = (P(("wide", "narrow"), None), P())
    out_specs = P(("wide", "narrow"), None)
    return jax.shard_map(
        on_device, mesh=mesh, in_specs=in_specs, out_specs=out_specs, check_vma=False
    )
```
